32 devices in a mesh: dp: 2 (over y), expert: 16 (over z, x, core).
Axes of the slice: x: 2, y: 2, z: 4, core: 2. Of those that a mesh axis runs over, the one named last changes fastest.
Arguments:
- grad_out: bfloat16 [1024, 4096], P(('dp', 'expert')), may hold values from -6 to 6
- expert_ids: int32 [1024, 8], P(('dp', 'expert')), may hold values from 0 to 15, all different within a row; in each aligned block of 32 rows (0 to 31, 32 to 63, ...) at most 20 rows name the same one
- route_weights: float32 [1024, 8], P(('dp', 'expert')), may hold values from 0.02 to 0.2
- hidden_act: bfloat16 [2, 16, 320, 1536], P('dp', 'expert'), may hold values from -6 to 6
- projection: bfloat16 [16, 1536, 256], P('expert', 'dp'), may hold values from -0.15625 to 0.15625
Outputs:
- projected_grad: bfloat16 [16, 4096, 256], P('expert', 'dp')
The draws below stay inside these ranges and needn't reach their ends.
Inputs may be any that keep to these rules, and one draw needn't show every extreme that they name: `expert_ids`: each row names 8 different experts. Among the 32 tokens of one device (aligned blocks of rows), no expert is named more than 20 times, a bound that some block reaches.
All inputs are finite; a program needn't handle non-finite values.
Results may differ from the reference program's by a relative error of at most 0.0058.
Values may be sent and summed in bfloat16 or wider, within the bound.
A program may use at most 64 MiB of HBM per device.

```python
import math
import jax
import jax.numpy as jnp
import numpy as np
from jax import lax

D = 4096
HID = 1536
TOPK = 8
RANK = 256
TOK_DEV = 32
EXPERTS = 16
CAP = 20
SLOTS = 320
ALL_TOKENS = 1024
N_DP = 2
N_EXPERT = 16


def block_levels(stream_key, shape, cuts, smallest, top_value):
    level, own = 1.0, jax.random.fold_in(stream_key, 6)
    for dim, shards_of in cuts:
        heights = jnp.exp(jax.random.uniform(jax.random.fold_in(own, dim), (shards_of,), jnp.float32, smallest / len(cuts), top_value / len(cuts)))
        level = level * jnp.repeat(heights, shape[dim] // shards_of).reshape([-1 if axis == dim else 1 for axis in range(len(shape))])
    return level


def routed_block(key, own, number, rows, number_of, top, bound, skew):
    order = jax.random.permutation(key, number_of)
    packed, ordinary = load_shares(number_of, rows * top, bound, skew, True), load_shares(number_of, rows * top, bound, skew, False)
    places = jnp.arange(number_of)

    def named(tallies, rotation):
        used = int((tallies > 0).sum())
        fixed = max(1, used // 4)
        moved = fixed + (places - fixed + rotation * (used - fixed)) % max(1, number_of - fixed)
        return jnp.zeros((number_of,), jnp.int32).at[order[jnp.where(places < fixed, places, moved)]].set(jnp.asarray(tallies, jnp.int32))

    tallies = jnp.where(number % 4 == 0, named(packed, number // 4), named(ordinary, number - number // 4 - 1))
    mixed = jax.random.permutation(jax.random.fold_in(own, 3), number_of)
    giver, sink = mixed[0:number_of // 2 * 2:2], mixed[1:number_of // 2 * 2:2]
    slack = jnp.minimum(tallies[giver] - 1, bound - tallies[sink]) // 2
    slack = jnp.where((giver == order[0]) | (sink == order[0]) | (tallies[sink] == 0), 0, jnp.maximum(slack, 0))
    moved = jax.random.randint(jax.random.fold_in(own, 4), (number_of // 2,), 0, 1 << 20) % (slack + 1)
    tallies = tallies.at[giver].add(-moved).at[sink].add(moved)
    items = jnp.searchsorted(jnp.cumsum(tallies), jnp.arange(rows * top), side="right").astype(jnp.int32)
    listing = items.reshape(top, rows).T
    listing = listing[jax.random.permutation(jax.random.fold_in(own, 1), rows)]
    rotation = jax.random.randint(jax.random.fold_in(own, 2), (rows, 1), 0, top)
    return jnp.take_along_axis(listing, (jnp.arange(top)[None, :] + rotation) % top, axis=1)


def load_shares(count, total, bound, skew, full):
    portions = [(1 << 20) // math.isqrt(rank ** skew) + 1 for rank in range(1, count + 1)]
    largest = bound if full else min(bound, max(-(-total // count), total * portions[0] // sum(portions)))
    least = 1 if total - largest >= count - 1 else 0
    given, spare = [largest] + [least] * (count - 1), total - largest - least * (count - 1)
    while spare > 0:
        free = [i for i in range(1, count) if given[i] < largest] or [i for i in range(1, count) if given[i] < bound]
        pool, remaining = sum([portions[i] for i in free]), spare
        for i in free:
            more = min(bound - given[i], max(1, remaining * portions[i] // pool), spare)
            given[i] = given[i] + more
            spare = spare - more
    return np.array(given)


def gaussian(key, extent, scale, limit, cuts=(), kind=jnp.bfloat16):
    drawn = scale * jax.random.normal(key, extent, jnp.float32)
    if cuts:
        drawn = drawn * block_levels(key, extent, cuts, -0.22, 0.18)
    return jnp.clip(drawn, -limit, limit).astype(kind)


def setup_inputs(seed: int = 0) -> dict:
    arg_keys = jax.random.split(jax.random.key(seed), 6)
    grad_out = gaussian(arg_keys[0], (ALL_TOKENS, D), 1.0, 6.0, ((0, 32),))
    expert_ids_keys = jax.random.split(jax.random.fold_in(arg_keys[1], 1), ALL_TOKENS // TOK_DEV)
    expert_ids_turns = jax.random.permutation(jax.random.fold_in(arg_keys[1], 3), ALL_TOKENS // TOK_DEV)
    expert_ids = jax.vmap(lambda own, number: routed_block(jax.random.fold_in(arg_keys[1], 2), own, number, TOK_DEV, EXPERTS, TOPK, CAP, 2))(expert_ids_keys, expert_ids_turns).reshape((ALL_TOKENS, TOPK))
    route_weights = jnp.clip(0.02 + 0.18 * jax.random.uniform(arg_keys[2], (ALL_TOKENS, TOPK), jnp.float32) ** block_levels(arg_keys[2], (ALL_TOKENS, TOPK), ((0, 32),), -0.2, 0.2), 0.02, 0.2)
    hidden_act = gaussian(arg_keys[3], (N_DP, EXPERTS, SLOTS, HID), 1.0, 6.0, ((0, 2), (1, 16)))
    projection = gaussian(arg_keys[4], (EXPERTS, HID, RANK), HID ** -0.5, 0.15625, ((0, 16), (1, 2)))
    return {"grad_out": grad_out, "expert_ids": expert_ids, "route_weights": route_weights, "hidden_act": hidden_act, "projection": projection}


def reference(grad_out, expert_ids, route_weights, hidden_act, projection):
    sources = N_DP * N_EXPERT
    per_source = TOK_DEV * TOPK
    routed = expert_ids.reshape(sources, per_source)
    onehot = (routed[:, :, None] == jnp.arange(EXPERTS, dtype=jnp.int32)[None, None, :]).astype(jnp.int32)
    earlier = jnp.cumsum(onehot, axis=1) - onehot
    position = jnp.sum(earlier * onehot, axis=2).astype(jnp.int32)
    slot = (routed * CAP + position).astype(jnp.int32)
    table = jnp.full((sources, EXPERTS * CAP), -1, jnp.int32)
    source_rows = jnp.broadcast_to(jnp.arange(sources, dtype=jnp.int32)[:, None], (sources, per_source))
    route_local = jnp.broadcast_to(jnp.arange(per_source, dtype=jnp.int32)[None, :], (sources, per_source))
    table = table.at[source_rows, slot].set(route_local)
    table = table.reshape(N_DP, N_EXPERT, EXPERTS, CAP)
    flat_weights = route_weights.reshape(-1)

    def one_expert(expert):
        total = jnp.zeros((D, RANK), jnp.float32)
        basis = lax.dynamic_index_in_dim(projection, expert, 0, keepdims=False)
        for replica in range(N_DP):
            picks = lax.dynamic_index_in_dim(table[replica], expert, 1, keepdims=False)
            source_base = ((replica * N_EXPERT + jnp.arange(N_EXPERT, dtype=jnp.int32)) * per_source)[:, None]
            valid = (picks >= 0).reshape(-1)
            route = (source_base + jnp.maximum(picks, 0)).reshape(-1).astype(jnp.int32)
            rows = grad_out[route // TOPK].astype(jnp.float32)
            weight = flat_weights[route]
            weighted = jnp.where(valid[:, None], weight[:, None] * rows, 0.0).astype(jnp.bfloat16)
            hidden = lax.dynamic_index_in_dim(hidden_act[replica], expert, 0, keepdims=False)
            reduced = jnp.dot(hidden, basis, preferred_element_type=jnp.float32).astype(jnp.bfloat16)
            total = total + jnp.dot(weighted.T, reduced, preferred_element_type=jnp.float32)
        return total.astype(jnp.bfloat16)

    return lax.map(one_expert, jnp.arange(EXPERTS, dtype=jnp.int32))
```

```python
import functools

import jax
import jax.numpy as jnp
from jax import lax
from jax.experimental import pallas as pl
from jax.experimental.pallas import tpu as pltpu
from jax.sharding import PartitionSpec as P

MESH = pl.DeviceIdType.MESH
PLANE = 4
TO_Y, TO_X, TO_UP, TO_DOWN, TO_CORE, TO_PAIR = range(6)


def gather_kernel(
    nz,
    g_ref, ids_ref, w_ref, h_ref, p_ref,
    out_ref,
    gbuf, msgs, meta, hbuf, pf, rt,
    send, recv, meta_send, meta_recv, side_send, side_recv, local,
):
    experts = nz * PLANE
    tokens = g_ref.shape[0]
    half = gbuf.shape[2]
    slots = hbuf.shape[0]
    capacity = slots // experts
    y = lax.axis_index("dp")
    me = lax.axis_index("expert")
    core = lax.rem(me, 2)
    x = lax.rem(lax.div(me, 2), 2)
    z = lax.div(me, PLANE)
    peer = 1 - y
    pair = z + 1 - 2 * lax.rem(z, 2)

    def place(ys, zs, xs, cs):
        return zs * (2 * PLANE) + ys * PLANE + xs * 2 + cs

    def device(zs, xs, cs):
        return (y, zs * PLANE + xs * 2 + cs)

    barrier = pltpu.get_barrier_semaphore()
    pl.semaphore_signal(barrier, inc=1, device_id=(peer, me), device_id_type=MESH)
    for k in range(1, experts):
        pl.semaphore_signal(
            barrier, inc=1, device_id=(y, lax.rem(me + k, experts)), device_id_type=MESH
        )

    own_columns = pl.ds(pl.multiple_of(y * half, half), half)
    peer_columns = pl.ds(pl.multiple_of(peer * half, half), half)
    own_place = place(y, z, x, core)
    copies = [
        pltpu.make_async_copy(g_ref.at[:, own_columns], gbuf.at[own_place], local.at[0]),
        pltpu.make_async_copy(h_ref.at[0, 0], hbuf, local.at[1]),
        pltpu.make_async_copy(p_ref.at[0], pf.at[y], local.at[2]),
    ]
    for copy in copies:
        copy.start()

    ids = jnp.concatenate([ids_ref[...]] * PLANE, axis=1)
    gains = jnp.concatenate([w_ref[...]] * PLANE, axis=1)
    expert_row = lax.broadcasted_iota(jnp.int32, (experts, 128), 0)
    weight = jnp.zeros((experts, 128), jnp.float32)
    named = jnp.zeros((experts, 128), jnp.float32)
    for k in range(ids_ref.shape[0]):
        hit = ids[k : k + 1] == expert_row
        weight = weight + jnp.where(hit, gains[k : k + 1], 0.0)
        named = named + jnp.where(hit, 1.0, 0.0)
    first = lax.broadcasted_iota(jnp.int32, (128, 128), 0)
    second = lax.broadcasted_iota(jnp.int32, (128, 128), 1)
    earlier = jnp.logical_and(first < second, first >= second - lax.rem(second, tokens))
    position = jnp.dot(
        named.astype(jnp.bfloat16),
        jnp.where(earlier, 1.0, 0.0).astype(jnp.bfloat16),
        preferred_element_type=jnp.float32,
    )
    base = (me * capacity + 1).astype(jnp.float32)
    number = jnp.where(named > 0.5, position + base, 0.0)
    lane_group = lax.div(lax.broadcasted_iota(jnp.int32, (experts, 128), 1), tokens)
    mine = lane_group == lax.rem(me, PLANE)
    msgs[:, 0, :] = jnp.where(mine, weight, 0.0)
    msgs[:, 1, :] = jnp.where(mine, number, 0.0)
    meta[pl.ds(me, 1)] = msgs[pl.ds(me, 1)]

    pl.semaphore_wait(barrier, experts)

    pending = []

    def send_block(src, where, way, target, condition=None):
        copy = pltpu.make_async_remote_copy(
            src_ref=src,
            dst_ref=gbuf.at[where],
            send_sem=send.at[way, where],
            recv_sem=recv.at[where],
            device_id=target,
            device_id_type=MESH,
        )
        pending.append((condition, copy))
        if condition is None:
            copy.start()
        else:
            pl.when(condition)(copy.start)

    def arrived(where):
        pltpu.make_async_remote_copy(
            src_ref=gbuf.at[where],
            dst_ref=gbuf.at[where],
            send_sem=send.at[0, where],
            recv_sem=recv.at[where],
            device_id=(peer, me),
            device_id_type=MESH,
        ).wait_recv()

    def both(a, b):
        return b if a is None else jnp.logical_and(a, b)

    to_x = device(z, 1 - x, core)
    to_core = device(z, x, 1 - core)
    to_up = device(lax.rem(z + 1, nz), x, core)
    to_down = device(lax.rem(z + nz - 1, nz), x, core)
    to_pair = device(pair, x, core)

    def side_copy(index, src, dst):
        return pltpu.make_async_remote_copy(
            src_ref=src, dst_ref=dst, send_sem=side_send.at[index], recv_sem=side_recv.at[index],
            device_id=(peer, me), device_id_type=MESH,
        )

    own = g_ref.at[:, own_columns]
    send_block(g_ref.at[:, peer_columns], own_place, TO_Y, (peer, me))
    send_block(own, own_place, TO_X, to_x)
    send_block(own, own_place, TO_UP, to_up, z < nz - 1)
    send_block(own, own_place, TO_DOWN, to_down, z > 0)
    send_block(own, own_place, TO_CORE, to_core)
    basis = side_copy(0, p_ref.at[0], pf.at[y])
    basis.start()
    notes = []
    for k in range(1, experts):
        target = lax.rem(me + k, experts)
        note = pltpu.make_async_remote_copy(
            src_ref=msgs.at[target], dst_ref=meta.at[me],
            send_sem=meta_send.at[k], recv_sem=meta_recv.at[me],
            device_id=(y, target), device_id_type=MESH,
        )
        note.start()
        notes.append(note)

    where = place(peer, z, x, core)
    arrived(where)
    block = gbuf.at[where]
    send_block(block, where, TO_X, to_x)
    send_block(block, where, TO_UP, to_up, z < nz - 1)
    send_block(block, where, TO_DOWN, to_down, z > 0)
    send_block(block, where, TO_CORE, to_core)

    def sides(distance):
        below = (z - distance, z - distance >= 0, TO_UP, to_up, z < nz - 1)
        above = (z + distance, z + distance < nz, TO_DOWN, to_down, z > 0)
        return below, above

    def from_column(distance, same):
        ys = y if same else peer
        for zs, valid, way, target, further in sides(distance):
            where = place(ys, zs, x, core)
            pl.when(valid)(functools.partial(arrived, where))
            block = gbuf.at[where]
            if distance < nz - 1:
                send_block(block, where, way, target, both(valid, further))
            crossing = valid
            if same and distance == 1:
                crossing = both(valid, zs != pair)
            send_block(block, where, TO_X, to_x, crossing)
            send_block(block, where, TO_CORE, to_core, valid)

    def from_x(distance, same):
        ys = y if same else peer
        if distance == 0:
            where = place(ys, z, 1 - x, core)
            arrived(where)
            if same:
                send_block(gbuf.at[where], where, TO_PAIR, to_pair)
            send_block(gbuf.at[where], where, TO_CORE, to_core)
            return
        for zs, valid, _, _, _ in sides(distance):
            if same and distance == 1:
                valid = both(valid, zs != pair)
            where = place(ys, zs, 1 - x, core)
            pl.when(valid)(functools.partial(arrived, where))
            send_block(gbuf.at[where], where, TO_CORE, to_core, valid)

    def from_pair():
        where = place(y, pair, 1 - x, core)
        arrived(where)
        send_block(gbuf.at[where], where, TO_CORE, to_core)

    def reduce_rows():
        for k in range(1, experts):
            source = lax.rem(me + k, experts)
            pltpu.make_async_remote_copy(
                src_ref=msgs.at[source], dst_ref=meta.at[source],
                send_sem=meta_send.at[k], recv_sem=meta_recv.at[source],
                device_id=(y, source), device_id_type=MESH,
            ).wait_recv()
        copies[1].wait()
        copies[2].wait()
        basis.wait_recv()
        depth = pf.shape[1]
        reduced = jnp.dot(
            hbuf[:, :depth], pf[0], preferred_element_type=jnp.float32
        ) + jnp.dot(hbuf[:, depth:], pf[1], preferred_element_type=jnp.float32)
        turned = reduced.T.astype(jnp.bfloat16)
        slot = lax.broadcasted_iota(jnp.int32, (slots, 128), 0).astype(jnp.float32) + 1.0
        for zs in range(nz):
            rows = jnp.sum(meta[PLANE * zs : PLANE * (zs + 1)], axis=0)
            chosen = jnp.where(slot == rows[1:2], 1.0, 0.0).astype(jnp.bfloat16)
            picked = jnp.dot(turned, chosen, preferred_element_type=jnp.float32)
            rt[y, zs] = (picked * rows[0:1]).astype(jnp.bfloat16)

    from_x(0, True)
    from_column(1, True)
    from_x(0, False)
    from_column(1, False)
    from_x(1, True)
    from_column(2, True)
    from_x(1, False)
    from_column(2, False)
    reduce_rows()
    factors = side_copy(1, rt.at[y], rt.at[y])
    factors.start()
    from_x(2, True)
    from_column(3, True)
    from_x(2, False)
    from_column(3, False)
    from_pair()
    from_x(3, True)
    from_x(3, False)

    copies[0].wait()
    factors.wait_recv()
    for xs in range(2):
        for ys in range(2):
            for zs in range(nz):
                arrived(place(ys, zs, xs, 1 - core))

    left = jnp.concatenate(
        [rt[ys, zs] for zs in range(nz) for ys in range(2)], axis=1
    )
    width = 512

    def columns_body(i, carry):
        columns = pl.ds(pl.multiple_of(i * width, width), width)
        right = gbuf[:, :, columns].reshape(gbuf.shape[0] * tokens, width)
        out_ref[:, columns] = jnp.dot(
            left, right, preferred_element_type=jnp.float32
        ).astype(jnp.bfloat16)
        return carry

    lax.fori_loop(0, half // width, columns_body, 0)

    for condition, copy in pending:
        if condition is None:
            copy.wait_send()
        else:
            pl.when(condition)(copy.wait_send)
    for copy in [basis, factors, *notes]:
        copy.wait_send()


def gathered(grad_out, expert_ids, route_weights, hidden_act, projection):
    experts = lax.axis_size("expert")
    nz = experts // PLANE
    tokens, features = grad_out.shape
    half = features // 2
    slots, hidden = hidden_act.shape[2:]
    rank = projection.shape[2]
    vmem = pl.BlockSpec(memory_space=pltpu.VMEM)
    anywhere = pl.BlockSpec(memory_space=pl.ANY)
    blocks = 2 * experts
    out = pl.pallas_call(
        functools.partial(gather_kernel, nz),
        out_shape=jax.ShapeDtypeStruct((rank, half), jnp.bfloat16),
        in_specs=[anywhere, vmem, vmem, anywhere, anywhere],
        out_specs=vmem,
        scratch_shapes=[
            pltpu.VMEM((blocks, tokens, half), jnp.bfloat16),
            pltpu.VMEM((experts, 2, 128), jnp.float32),
            pltpu.VMEM((experts, 2, 128), jnp.float32),
            pltpu.VMEM((slots, hidden), jnp.bfloat16),
            pltpu.VMEM((2, hidden // 2, rank), jnp.bfloat16),
            pltpu.VMEM((2, nz, rank, PLANE * tokens), jnp.bfloat16),
            pltpu.SemaphoreType.DMA((6, blocks)),
            pltpu.SemaphoreType.DMA((blocks,)),
            pltpu.SemaphoreType.DMA((experts,)),
            pltpu.SemaphoreType.DMA((experts,)),
            pltpu.SemaphoreType.DMA((2,)),
            pltpu.SemaphoreType.DMA((2,)),
            pltpu.SemaphoreType.DMA((3,)),
        ],
        compiler_params=pltpu.CompilerParams(
            collective_id=0, has_side_effects=True, vmem_limit_bytes=60 * 1024 * 1024
        ),
        cost_estimate=pl.CostEstimate(
            flops=2 * rank * (half * blocks * tokens + slots * hidden),
            bytes_accessed=4 * 1024 * 1024,
            transcendentals=0,
        ),
        name="gather_project",
    )(grad_out, expert_ids.T, route_weights.T, hidden_act, projection)
    return out.T[None]


def exchanged(grad_out, expert_ids, route_weights, hidden_act, projection):
    token_count, width = grad_out.shape
    top_count = expert_ids.shape[1]
    expert_count = lax.axis_size("expert")
    slot_count = hidden_act.shape[2]
    capacity = slot_count // expert_count
    onehot = (
        expert_ids[:, :, None] == jnp.arange(expert_count, dtype=jnp.int32)
    ).astype(jnp.float32)
    named = jnp.sum(onehot, axis=1)
    order = jnp.arange(token_count)
    before = (order[:, None] > order[None, :]).astype(jnp.float32)
    earlier = jnp.dot(before, named, preferred_element_type=jnp.float32)
    position = jnp.sum(onehot * earlier[:, None, :], axis=2).astype(jnp.int32)
    slot = (expert_ids * capacity + position).reshape(-1)
    table = jnp.full((expert_count * capacity,), -1, jnp.int32)
    table = table.at[slot].set(jnp.arange(token_count * top_count, dtype=jnp.int32))
    picked = jnp.maximum(table, 0)
    rows = grad_out[picked // top_count].astype(jnp.float32)
    weight = route_weights.reshape(-1)[picked]
    weighted = jnp.where((table >= 0)[:, None], weight[:, None] * rows, 0.0)
    outgoing = weighted.astype(jnp.bfloat16).reshape(expert_count, capacity, width)
    reduced = jnp.dot(
        hidden_act[0, 0],
        lax.all_gather(projection[0], "dp", axis=0, tiled=True),
        preferred_element_type=jnp.float32,
    ).astype(jnp.bfloat16)
    arrived = lax.all_to_all(outgoing, "expert", split_axis=0, concat_axis=0, tiled=True)
    share = lax.psum_scatter(
        lax.dot_general(
            arrived.reshape(slot_count, width),
            reduced,
            (((0,), (0,)), ((), ())),
            preferred_element_type=jnp.float32,
        ),
        "dp",
        scatter_dimension=0,
        tiled=True,
    )
    return share.astype(jnp.bfloat16)[None]


def solution(mesh):
    in_specs = (
        P(("dp", "expert"), None),
        P(("dp", "expert"), None),
        P(("dp", "expert"), None),
        P("dp", "expert", None, None),
        P("expert", "dp", None),
    )
    out_specs = P("expert", "dp", None)
    small = mesh.shape["dp"] == 2 and mesh.shape["expert"] == 16
    return jax.shard_map(
        gathered if small else exchanged,
        mesh=mesh, in_specs=in_specs, out_specs=out_specs, check_vma=False,
    )
```

```python
import functools

import jax
import jax.numpy as jnp
from jax import lax
from jax.experimental import pallas as pl
from jax.experimental.pallas import tpu as pltpu
from jax.sharding import PartitionSpec as P

MESH = pl.DeviceIdType.MESH
PLANE = 4
PARTS, LAG, PAIR_AT, REDUCE_AT = 1, 2, 6, 5
TO_Y, TO_X, TO_UP, TO_DOWN, TO_CORE, TO_PAIR = range(6)


def gather_kernel(
    nz,
    g_ref, ids_ref, w_ref, h_ref, p_ref,
    out_ref,
    gbuf, msgs, meta, hbuf, pf, rt,
    send, recv, meta_send, meta_recv, side_send, side_recv, local,
):
    experts = nz * PLANE
    tokens = g_ref.shape[0]
    piece = gbuf.shape[3]
    slots = hbuf.shape[0]
    capacity = slots // experts
    y = lax.axis_index("dp")
    me = lax.axis_index("expert")
    core = lax.rem(me, 2)
    x = lax.rem(lax.div(me, 2), 2)
    z = lax.div(me, PLANE)
    peer = 1 - y
    pair = z + 1 - 2 * lax.rem(z, 2)

    def place(ys, zs, xs, cs):
        return zs * (2 * PLANE) + ys * PLANE + xs * 2 + cs

    def device(zs, xs, cs):
        return (y, zs * PLANE + xs * 2 + cs)

    barrier = pltpu.get_barrier_semaphore()
    pl.semaphore_signal(barrier, inc=1, device_id=(peer, me), device_id_type=MESH)
    for k in range(1, experts):
        pl.semaphore_signal(
            barrier, inc=1, device_id=(y, lax.rem(me + k, experts)), device_id_type=MESH
        )

    own_place = place(y, z, x, core)

    def columns_of(replica, part):
        return pl.ds(pl.multiple_of(replica * (PARTS * piece) + part * piece, piece), piece)

    copies = [
        pltpu.make_async_copy(h_ref.at[0, 0], hbuf, local.at[0]),
        pltpu.make_async_copy(p_ref.at[0], pf.at[y], local.at[1]),
    ]
    for part in range(PARTS):
        copies.append(
            pltpu.make_async_copy(
                g_ref.at[:, columns_of(y, part)], gbuf.at[part, own_place], local.at[2 + part]
            )
        )
    for copy in copies:
        copy.start()

    pl.semaphore_wait(barrier, experts)

    pending = []

    def send_block(src, where, part, way, target, condition=None):
        copy = pltpu.make_async_remote_copy(
            src_ref=gbuf.at[part, where] if src is None else src,
            dst_ref=gbuf.at[part, where],
            send_sem=send.at[way, part, where],
            recv_sem=recv.at[part, where],
            device_id=target,
            device_id_type=MESH,
        )
        pending.append((condition, copy))
        if condition is None:
            copy.start()
        else:
            pl.when(condition)(copy.start)

    def arrived(where, part):
        pltpu.make_async_remote_copy(
            src_ref=gbuf.at[part, where],
            dst_ref=gbuf.at[part, where],
            send_sem=send.at[0, part, where],
            recv_sem=recv.at[part, where],
            device_id=(peer, me),
            device_id_type=MESH,
        ).wait_recv()

    def both(a, b):
        return b if a is None else jnp.logical_and(a, b)

    to_x = device(z, 1 - x, core)
    to_core = device(z, x, 1 - core)
    to_up = device(lax.rem(z + 1, nz), x, core)
    to_down = device(lax.rem(z + nz - 1, nz), x, core)
    to_pair = device(pair, x, core)

    def side_copy(index, src, dst):
        return pltpu.make_async_remote_copy(
            src_ref=src, dst_ref=dst, send_sem=side_send.at[index], recv_sem=side_recv.at[index],
            device_id=(peer, me), device_id_type=MESH,
        )

    basis = side_copy(0, p_ref.at[0], pf.at[y])
    factors = side_copy(1, rt.at[y], rt.at[y])
    def write_notes():
        ids = jnp.concatenate([ids_ref[...]] * PLANE, axis=1)
        gains = jnp.concatenate([w_ref[...]] * PLANE, axis=1)
        expert_row = lax.broadcasted_iota(jnp.int32, (experts, 128), 0)
        weight = jnp.zeros((experts, 128), jnp.float32)
        named = jnp.zeros((experts, 128), jnp.float32)
        for k in range(ids_ref.shape[0]):
            hit = ids[k : k + 1] == expert_row
            weight = weight + jnp.where(hit, gains[k : k + 1], 0.0)
            named = named + jnp.where(hit, 1.0, 0.0)
        first = lax.broadcasted_iota(jnp.int32, (128, 128), 0)
        second = lax.broadcasted_iota(jnp.int32, (128, 128), 1)
        earlier = jnp.logical_and(first < second, first >= second - lax.rem(second, tokens))
        position = jnp.dot(
            named.astype(jnp.bfloat16),
            jnp.where(earlier, 1.0, 0.0).astype(jnp.bfloat16),
            preferred_element_type=jnp.float32,
        )
        base = (me * capacity + 1).astype(jnp.float32)
        number = jnp.where(named > 0.5, position + base, 0.0)
        lane_group = lax.div(lax.broadcasted_iota(jnp.int32, (experts, 128), 1), tokens)
        mine = lane_group == lax.rem(me, PLANE)
        msgs[:, 0, :] = jnp.where(mine, weight, 0.0)
        msgs[:, 1, :] = jnp.where(mine, number, 0.0)
        meta[pl.ds(me, 1)] = msgs[pl.ds(me, 1)]

    notes = []

    def send_notes():
        for k in range(1, experts):
            target = lax.rem(me + k, experts)
            note = pltpu.make_async_remote_copy(
                src_ref=msgs.at[target], dst_ref=meta.at[me],
                send_sem=meta_send.at[k], recv_sem=meta_recv.at[me],
                device_id=(y, target), device_id_type=MESH,
            )
            note.start()
            notes.append(note)

    def sides(distance):
        below = (z - distance, z - distance >= 0, TO_UP, to_up, z < nz - 1)
        above = (z + distance, z + distance < nz, TO_DOWN, to_down, z > 0)
        return below, above

    def from_column(distance, same, part):
        ys = y if same else peer
        if distance == 0:
            where = place(ys, z, x, core)
            src = None
            if same:
                src = g_ref.at[:, columns_of(y, part)]
                send_block(g_ref.at[:, columns_of(peer, part)], where, part, TO_Y, (peer, me))
            else:
                arrived(where, part)
            send_block(src, where, part, TO_X, to_x)
            send_block(src, where, part, TO_UP, to_up, z < nz - 1)
            send_block(src, where, part, TO_DOWN, to_down, z > 0)
            send_block(src, where, part, TO_CORE, to_core)
            return
        for zs, valid, way, target, further in sides(distance):
            where = place(ys, zs, x, core)
            pl.when(valid)(functools.partial(arrived, where, part))
            if distance < nz - 1:
                send_block(None, where, part, way, target, both(valid, further))
            crossing = valid
            if same and distance == 1:
                crossing = both(valid, zs != pair)
            send_block(None, where, part, TO_X, to_x, crossing)
            send_block(None, where, part, TO_CORE, to_core, valid)

    def from_x(distance, same, part):
        ys = y if same else peer
        if distance == 0:
            where = place(ys, z, 1 - x, core)
            arrived(where, part)
            send_block(None, where, part, TO_CORE, to_core)
            return
        for zs, valid, _, _, _ in sides(distance):
            if same and distance == 1:
                valid = both(valid, zs != pair)
            where = place(ys, zs, 1 - x, core)
            pl.when(valid)(functools.partial(arrived, where, part))
            send_block(None, where, part, TO_CORE, to_core, valid)

    def to_neighbour_pair():
        for part in range(PARTS):
            send_block(None, place(y, z, 1 - x, core), part, TO_PAIR, to_pair)

    def from_pair():
        for part in range(PARTS):
            where = place(y, pair, 1 - x, core)
            arrived(where, part)
            send_block(None, where, part, TO_CORE, to_core)

    def reduce_rows():
        for k in range(1, experts):
            source = lax.rem(me + k, experts)
            pltpu.make_async_remote_copy(
                src_ref=msgs.at[source], dst_ref=meta.at[source],
                send_sem=meta_send.at[k], recv_sem=meta_recv.at[source],
                device_id=(y, source), device_id_type=MESH,
            ).wait_recv()
        copies[0].wait()
        copies[1].wait()
        basis.wait_recv()
        depth = pf.shape[1]
        reduced = jnp.dot(
            hbuf[:, :depth], pf[0], preferred_element_type=jnp.float32
        ) + jnp.dot(hbuf[:, depth:], pf[1], preferred_element_type=jnp.float32)
        turned = reduced.T.astype(jnp.bfloat16)
        slot = lax.broadcasted_iota(jnp.int32, (slots, 128), 0).astype(jnp.float32) + 1.0
        for zs in range(nz):
            rows = jnp.sum(meta[PLANE * zs : PLANE * (zs + 1)], axis=0)
            chosen = jnp.where(slot == rows[1:2], 1.0, 0.0).astype(jnp.bfloat16)
            picked = jnp.dot(turned, chosen, preferred_element_type=jnp.float32)
            rt[y, zs] = (picked * rows[0:1]).astype(jnp.bfloat16)

    steps = [
        (distance, same, part)
        for distance in range(nz)
        for same in (True, False)
        for part in range(PARTS)
    ]
    for i in range(len(steps) + LAG):
        if i < len(steps):
            from_column(*steps[i])
        if i >= LAG:
            from_x(*steps[i - LAG])
        if i == PARTS - 1:
            write_notes()
            send_notes()
        if i == 2 * PARTS - 1:
            basis.start()
        if i == PAIR_AT * PARTS:
            to_neighbour_pair()
        if i == REDUCE_AT * PARTS:
            reduce_rows()
            factors.start()
    from_pair()

    for copy in copies[2:]:
        copy.wait()
    factors.wait_recv()
    for part in range(PARTS):
        for xs in range(2):
            for ys in range(2):
                for zs in range(nz):
                    arrived(place(ys, zs, xs, 1 - core), part)

    left = jnp.concatenate(
        [rt[ys, zs] for zs in range(nz) for ys in range(2)], axis=1
    )
    width = 512
    for part in range(PARTS):

        def columns_body(i, carry, part=part):
            offset = pl.multiple_of(i * width, width)
            right = gbuf[part, :, :, pl.ds(offset, width)].reshape(-1, width)
            out_ref[:, pl.ds(part * piece + offset, width)] = jnp.dot(
                left, right, preferred_element_type=jnp.float32
            ).astype(jnp.bfloat16)
            return carry

        lax.fori_loop(0, piece // width, columns_body, 0)

    for condition, copy in pending:
        if condition is None:
            copy.wait_send()
        else:
            pl.when(condition)(copy.wait_send)
    for copy in [basis, factors, *notes]:
        copy.wait_send()


def gathered(grad_out, expert_ids, route_weights, hidden_act, projection):
    experts = lax.axis_size("expert")
    nz = experts // PLANE
    tokens, features = grad_out.shape
    half = features // 2
    slots, hidden = hidden_act.shape[2:]
    rank = projection.shape[2]
    vmem = pl.BlockSpec(memory_space=pltpu.VMEM)
    anywhere = pl.BlockSpec(memory_space=pl.ANY)
    blocks = 2 * experts
    out = pl.pallas_call(
        functools.partial(gather_kernel, nz),
        out_shape=jax.ShapeDtypeStruct((rank, half), jnp.bfloat16),
        in_specs=[anywhere, vmem, vmem, anywhere, anywhere],
        out_specs=vmem,
        scratch_shapes=[
            pltpu.VMEM((PARTS, blocks, tokens, half // PARTS), jnp.bfloat16),
            pltpu.VMEM((experts, 2, 128), jnp.float32),
            pltpu.VMEM((experts, 2, 128), jnp.float32),
            pltpu.VMEM((slots, hidden), jnp.bfloat16),
            pltpu.VMEM((2, hidden // 2, rank), jnp.bfloat16),
            pltpu.VMEM((2, nz, rank, PLANE * tokens), jnp.bfloat16),
            pltpu.SemaphoreType.DMA((6, PARTS, blocks)),
            pltpu.SemaphoreType.DMA((PARTS, blocks)),
            pltpu.SemaphoreType.DMA((experts,)),
            pltpu.SemaphoreType.DMA((experts,)),
            pltpu.SemaphoreType.DMA((2,)),
            pltpu.SemaphoreType.DMA((2,)),
            pltpu.SemaphoreType.DMA((2 + PARTS,)),
        ],
        compiler_params=pltpu.CompilerParams(
            collective_id=0, has_side_effects=True, vmem_limit_bytes=60 * 1024 * 1024
        ),
        cost_estimate=pl.CostEstimate(
            flops=2 * rank * (half * blocks * tokens + slots * hidden),
            bytes_accessed=4 * 1024 * 1024,
            transcendentals=0,
        ),
        name="gather_project",
    )(grad_out, expert_ids.T, route_weights.T, hidden_act, projection)
    return out.T[None]


def exchanged(grad_out, expert_ids, route_weights, hidden_act, projection):
    token_count, width = grad_out.shape
    top_count = expert_ids.shape[1]
    expert_count = lax.axis_size("expert")
    slot_count = hidden_act.shape[2]
    capacity = slot_count // expert_count
    onehot = (
        expert_ids[:, :, None] == jnp.arange(expert_count, dtype=jnp.int32)
    ).astype(jnp.float32)
    named = jnp.sum(onehot, axis=1)
    order = jnp.arange(token_count)
    before = (order[:, None] > order[None, :]).astype(jnp.float32)
    earlier = jnp.dot(before, named, preferred_element_type=jnp.float32)
    position = jnp.sum(onehot * earlier[:, None, :], axis=2).astype(jnp.int32)
    slot = (expert_ids * capacity + position).reshape(-1)
    table = jnp.full((expert_count * capacity,), -1, jnp.int32)
    table = table.at[slot].set(jnp.arange(token_count * top_count, dtype=jnp.int32))
    picked = jnp.maximum(table, 0)
    rows = grad_out[picked // top_count].astype(jnp.float32)
    weight = route_weights.reshape(-1)[picked]
    weighted = jnp.where((table >= 0)[:, None], weight[:, None] * rows, 0.0)
    outgoing = weighted.astype(jnp.bfloat16).reshape(expert_count, capacity, width)
    reduced = jnp.dot(
        hidden_act[0, 0],
        lax.all_gather(projection[0], "dp", axis=0, tiled=True),
        preferred_element_type=jnp.float32,
    ).astype(jnp.bfloat16)
    arrived = lax.all_to_all(outgoing, "expert", split_axis=0, concat_axis=0, tiled=True)
    share = lax.psum_scatter(
        lax.dot_general(
            arrived.reshape(slot_count, width),
            reduced,
            (((0,), (0,)), ((), ())),
            preferred_element_type=jnp.float32,
        ),
        "dp",
        scatter_dimension=0,
        tiled=True,
    )
    return share.astype(jnp.bfloat16)[None]


def solution(mesh):
    in_specs = (
        P(("dp", "expert"), None),
        P(("dp", "expert"), None),
        P(("dp", "expert"), None),
        P("dp", "expert", None, None),
        P("expert", "dp", None),
    )
    out_specs = P("expert", "dp", None)
    small = mesh.shape["dp"] == 2 and mesh.shape["expert"] == 16
    return jax.shard_map(
        gathered if small else exchanged,
        mesh=mesh, in_specs=in_specs, out_specs=out_specs, check_vma=False,
    )
```

```python
import functools

import jax
import jax.numpy as jnp
from jax import lax
from jax.experimental import pallas as pl
from jax.experimental.pallas import tpu as pltpu
from jax.sharding import PartitionSpec as P

MESH = pl.DeviceIdType.MESH
PLANE = 4
PARTS, LAG, PAIR_AT, REDUCE_AT = 1, 2, 6, 5
TO_Y, TO_X, TO_UP, TO_DOWN, TO_CORE, TO_PAIR = range(6)


def gather_kernel(
    nz,
    g_ref, ids_ref, w_ref, h_ref, p_ref,
    out_ref,
    gbuf, msgs, meta, hbuf, pf, rt,
    send, recv, meta_send, meta_recv, side_send, side_recv, local,
):
    experts = nz * PLANE
    tokens = g_ref.shape[0]
    piece = gbuf.shape[3]
    slots = hbuf.shape[0]
    capacity = slots // experts
    y = lax.axis_index("dp")
    me = lax.axis_index("expert")
    core = lax.rem(me, 2)
    x = lax.rem(lax.div(me, 2), 2)
    z = lax.div(me, PLANE)
    peer = 1 - y
    pair = z + 1 - 2 * lax.rem(z, 2)

    def place(ys, zs, xs, cs):
        return zs * (2 * PLANE) + ys * PLANE + xs * 2 + cs

    def device(zs, xs, cs):
        return (y, zs * PLANE + xs * 2 + cs)

    barrier = pltpu.get_barrier_semaphore()
    pl.semaphore_signal(barrier, inc=1, device_id=(peer, me), device_id_type=MESH)
    for k in range(1, experts):
        pl.semaphore_signal(
            barrier, inc=1, device_id=(y, lax.rem(me + k, experts)), device_id_type=MESH
        )

    own_place = place(y, z, x, core)

    def columns_of(replica, part):
        return pl.ds(pl.multiple_of(replica * (PARTS * piece) + part * piece, piece), piece)

    copies = [
        pltpu.make_async_copy(h_ref.at[0, 0], hbuf, local.at[0]),
        pltpu.make_async_copy(p_ref.at[0], pf.at[y], local.at[1]),
    ]
    for part in range(PARTS):
        copies.append(
            pltpu.make_async_copy(
                g_ref.at[:, columns_of(y, part)], gbuf.at[part, own_place], local.at[2 + part]
            )
        )
    for copy in copies:
        copy.start()

    pl.semaphore_wait(barrier, experts)

    pending = []

    def send_block(src, where, part, way, target, condition=None):
        copy = pltpu.make_async_remote_copy(
            src_ref=gbuf.at[part, where] if src is None else src,
            dst_ref=gbuf.at[part, where],
            send_sem=send.at[way, part, where],
            recv_sem=recv.at[part, where],
            device_id=target,
            device_id_type=MESH,
        )
        pending.append((condition, copy))
        if condition is None:
            copy.start()
        else:
            pl.when(condition)(copy.start)

    def arrived(where, part):
        pltpu.make_async_remote_copy(
            src_ref=gbuf.at[part, where],
            dst_ref=gbuf.at[part, where],
            send_sem=send.at[0, part, where],
            recv_sem=recv.at[part, where],
            device_id=(peer, me),
            device_id_type=MESH,
        ).wait_recv()

    def both(a, b):
        return b if a is None else jnp.logical_and(a, b)

    to_x = device(z, 1 - x, core)
    to_core = device(z, x, 1 - core)
    to_up = device(lax.rem(z + 1, nz), x, core)
    to_down = device(lax.rem(z + nz - 1, nz), x, core)
    to_pair = device(pair, x, core)

    def side_copy(index, src, dst):
        return pltpu.make_async_remote_copy(
            src_ref=src, dst_ref=dst, send_sem=side_send.at[index], recv_sem=side_recv.at[index],
            device_id=(peer, me), device_id_type=MESH,
        )

    basis = side_copy(0, p_ref.at[0], pf.at[y])
    factors = side_copy(1, rt.at[y], rt.at[y])
    def write_notes():
        ids = jnp.concatenate([ids_ref[...]] * PLANE, axis=1)
        gains = jnp.concatenate([w_ref[...]] * PLANE, axis=1)
        expert_row = lax.broadcasted_iota(jnp.int32, (experts, 128), 0)
        weight = jnp.zeros((experts, 128), jnp.float32)
        named = jnp.zeros((experts, 128), jnp.float32)
        for k in range(ids_ref.shape[0]):
            hit = ids[k : k + 1] == expert_row
            weight = weight + jnp.where(hit, gains[k : k + 1], 0.0)
            named = named + jnp.where(hit, 1.0, 0.0)
        first = lax.broadcasted_iota(jnp.int32, (128, 128), 0)
        second = lax.broadcasted_iota(jnp.int32, (128, 128), 1)
        earlier = jnp.logical_and(first < second, first >= second - lax.rem(second, tokens))
        position = jnp.dot(
            named.astype(jnp.bfloat16),
            jnp.where(earlier, 1.0, 0.0).astype(jnp.bfloat16),
            preferred_element_type=jnp.float32,
        )
        base = (me * capacity + 1).astype(jnp.float32)
        number = jnp.where(named > 0.5, position + base, 0.0)
        lane_group = lax.div(lax.broadcasted_iota(jnp.int32, (experts, 128), 1), tokens)
        mine = lane_group == lax.rem(me, PLANE)
        msgs[:, 0, :] = jnp.where(mine, weight, 0.0)
        msgs[:, 1, :] = jnp.where(mine, number, 0.0)
        meta[pl.ds(me, 1)] = msgs[pl.ds(me, 1)]

    notes = []

    def send_notes():
        for k in range(1, experts):
            target = lax.rem(me + k, experts)
            note = pltpu.make_async_remote_copy(
                src_ref=msgs.at[target], dst_ref=meta.at[me],
                send_sem=meta_send.at[k], recv_sem=meta_recv.at[me],
                device_id=(y, target), device_id_type=MESH,
            )
            note.start()
            notes.append(note)

    def sides(distance):
        below = (z - distance, z - distance >= 0, TO_UP, to_up, z < nz - 1)
        above = (z + distance, z + distance < nz, TO_DOWN, to_down, z > 0)
        return below, above

    def from_column(distance, same, part):
        ys = y if same else peer
        if distance == 0:
            where = place(ys, z, x, core)
            src = None
            if same:
                src = g_ref.at[:, columns_of(y, part)]
                send_block(g_ref.at[:, columns_of(peer, part)], where, part, TO_Y, (peer, me))
            else:
                arrived(where, part)
            send_block(src, where, part, TO_UP, to_up, z < nz - 1)
            send_block(src, where, part, TO_DOWN, to_down, z > 0)
            send_block(src, where, part, TO_X, to_x)
            send_block(src, where, part, TO_CORE, to_core)
            return
        for zs, valid, way, target, further in sides(distance):
            where = place(ys, zs, x, core)
            pl.when(valid)(functools.partial(arrived, where, part))
            if distance < nz - 1:
                send_block(None, where, part, way, target, both(valid, further))
            crossing = valid
            if same and distance == 1:
                crossing = both(valid, zs != pair)
            send_block(None, where, part, TO_X, to_x, crossing)
            send_block(None, where, part, TO_CORE, to_core, valid)

    def from_x(distance, same, part):
        ys = y if same else peer
        if distance == 0:
            where = place(ys, z, 1 - x, core)
            arrived(where, part)
            send_block(None, where, part, TO_CORE, to_core)
            return
        for zs, valid, _, _, _ in sides(distance):
            if same and distance == 1:
                valid = both(valid, zs != pair)
            where = place(ys, zs, 1 - x, core)
            pl.when(valid)(functools.partial(arrived, where, part))
            send_block(None, where, part, TO_CORE, to_core, valid)

    def to_neighbour_pair():
        for part in range(PARTS):
            send_block(None, place(y, z, 1 - x, core), part, TO_PAIR, to_pair)

    def from_pair():
        for part in range(PARTS):
            where = place(y, pair, 1 - x, core)
            arrived(where, part)
            send_block(None, where, part, TO_CORE, to_core)

    def reduce_rows():
        for k in range(1, experts):
            source = lax.rem(me + k, experts)
            pltpu.make_async_remote_copy(
                src_ref=msgs.at[source], dst_ref=meta.at[source],
                send_sem=meta_send.at[k], recv_sem=meta_recv.at[source],
                device_id=(y, source), device_id_type=MESH,
            ).wait_recv()
        copies[0].wait()
        copies[1].wait()
        basis.wait_recv()
        depth = pf.shape[1]
        reduced = jnp.dot(
            hbuf[:, :depth], pf[0], preferred_element_type=jnp.float32
        ) + jnp.dot(hbuf[:, depth:], pf[1], preferred_element_type=jnp.float32)
        turned = reduced.T.astype(jnp.bfloat16)
        slot = lax.broadcasted_iota(jnp.int32, (slots, 128), 0).astype(jnp.float32) + 1.0
        for zs in range(nz):
            rows = jnp.sum(meta[PLANE * zs : PLANE * (zs + 1)], axis=0)
            chosen = jnp.where(slot == rows[1:2], 1.0, 0.0).astype(jnp.bfloat16)
            picked = jnp.dot(turned, chosen, preferred_element_type=jnp.float32)
            rt[y, zs] = (picked * rows[0:1]).astype(jnp.bfloat16)

    steps = [
        (distance, same, part)
        for distance in range(nz)
        for same in (True, False)
        for part in range(PARTS)
    ]
    for i in range(len(steps) + LAG):
        if i < len(steps):
            from_column(*steps[i])
        if i >= LAG:
            from_x(*steps[i - LAG])
        if i == PARTS - 1:
            write_notes()
            send_notes()
        if i == 2 * PARTS - 1:
            basis.start()
        if i == PAIR_AT * PARTS:
            to_neighbour_pair()
        if i == REDUCE_AT * PARTS:
            reduce_rows()
            factors.start()
    from_pair()

    for copy in copies[2:]:
        copy.wait()
    factors.wait_recv()
    for part in range(PARTS):
        for xs in range(2):
            for ys in range(2):
                for zs in range(nz):
                    arrived(place(ys, zs, xs, 1 - core), part)

    left = jnp.concatenate(
        [rt[ys, zs] for zs in range(nz) for ys in range(2)], axis=1
    )
    width = piece
    for part in range(PARTS):

        def columns_body(i, carry, part=part):
            offset = pl.multiple_of(i * width, width)
            right = gbuf[part, :, :, pl.ds(offset, width)].reshape(-1, width)
            out_ref[:, pl.ds(part * piece + offset, width)] = jnp.dot(
                left, right, preferred_element_type=jnp.float32
            ).astype(jnp.bfloat16)
            return carry

        lax.fori_loop(0, piece // width, columns_body, 0)

    for condition, copy in pending:
        if condition is None:
            copy.wait_send()
        else:
            pl.when(condition)(copy.wait_send)
    for copy in [basis, factors, *notes]:
        copy.wait_send()


def gathered(grad_out, expert_ids, route_weights, hidden_act, projection):
    experts = lax.axis_size("expert")
    nz = experts // PLANE
    tokens, features = grad_out.shape
    half = features // 2
    slots, hidden = hidden_act.shape[2:]
    rank = projection.shape[2]
    vmem = pl.BlockSpec(memory_space=pltpu.VMEM)
    anywhere = pl.BlockSpec(memory_space=pl.ANY)
    blocks = 2 * experts
    out = pl.pallas_call(
        functools.partial(gather_kernel, nz),
        out_shape=jax.ShapeDtypeStruct((rank, half), jnp.bfloat16),
        in_specs=[anywhere, vmem, vmem, anywhere, anywhere],
        out_specs=vmem,
        scratch_shapes=[
            pltpu.VMEM((PARTS, blocks, tokens, half // PARTS), jnp.bfloat16),
            pltpu.VMEM((experts, 2, 128), jnp.float32),
            pltpu.VMEM((experts, 2, 128), jnp.float32),
            pltpu.VMEM((slots, hidden), jnp.bfloat16),
            pltpu.VMEM((2, hidden // 2, rank), jnp.bfloat16),
            pltpu.VMEM((2, nz, rank, PLANE * tokens), jnp.bfloat16),
            pltpu.SemaphoreType.DMA((6, PARTS, blocks)),
            pltpu.SemaphoreType.DMA((PARTS, blocks)),
            pltpu.SemaphoreType.DMA((experts,)),
            pltpu.SemaphoreType.DMA((experts,)),
            pltpu.SemaphoreType.DMA((2,)),
            pltpu.SemaphoreType.DMA((2,)),
            pltpu.SemaphoreType.DMA((2 + PARTS,)),
        ],
        compiler_params=pltpu.CompilerParams(
            collective_id=0, has_side_effects=True, vmem_limit_bytes=60 * 1024 * 1024
        ),
        cost_estimate=pl.CostEstimate(
            flops=2 * rank * (half * blocks * tokens + slots * hidden),
            bytes_accessed=4 * 1024 * 1024,
            transcendentals=0,
        ),
        name="gather_project",
    )(grad_out, expert_ids.T, route_weights.T, hidden_act, projection)
    return out.T[None]


def exchanged(grad_out, expert_ids, route_weights, hidden_act, projection):
    token_count, width = grad_out.shape
    top_count = expert_ids.shape[1]
    expert_count = lax.axis_size("expert")
    slot_count = hidden_act.shape[2]
    capacity = slot_count // expert_count
    onehot = (
        expert_ids[:, :, None] == jnp.arange(expert_count, dtype=jnp.int32)
    ).astype(jnp.float32)
    named = jnp.sum(onehot, axis=1)
    order = jnp.arange(token_count)
    before = (order[:, None] > order[None, :]).astype(jnp.float32)
    earlier = jnp.dot(before, named, preferred_element_type=jnp.float32)
    position = jnp.sum(onehot * earlier[:, None, :], axis=2).astype(jnp.int32)
    slot = (expert_ids * capacity + position).reshape(-1)
    table = jnp.full((expert_count * capacity,), -1, jnp.int32)
    table = table.at[slot].set(jnp.arange(token_count * top_count, dtype=jnp.int32))
    picked = jnp.maximum(table, 0)
    rows = grad_out[picked // top_count].astype(jnp.float32)
    weight = route_weights.reshape(-1)[picked]
    weighted = jnp.where((table >= 0)[:, None], weight[:, None] * rows, 0.0)
    outgoing = weighted.astype(jnp.bfloat16).reshape(expert_count, capacity, width)
    reduced = jnp.dot(
        hidden_act[0, 0],
        lax.all_gather(projection[0], "dp", axis=0, tiled=True),
        preferred_element_type=jnp.float32,
    ).astype(jnp.bfloat16)
    arrived = lax.all_to_all(outgoing, "expert", split_axis=0, concat_axis=0, tiled=True)
    share = lax.psum_scatter(
        lax.dot_general(
            arrived.reshape(slot_count, width),
            reduced,
            (((0,), (0,)), ((), ())),
            preferred_element_type=jnp.float32,
        ),
        "dp",
        scatter_dimension=0,
        tiled=True,
    )
    return share.astype(jnp.bfloat16)[None]


def solution(mesh):
    in_specs = (
        P(("dp", "expert"), None),
        P(("dp", "expert"), None),
        P(("dp", "expert"), None),
        P("dp", "expert", None, None),
        P("expert", "dp", None),
    )
    out_specs = P("expert", "dp", None)
    small = mesh.shape["dp"] == 2 and mesh.shape["expert"] == 16
    return jax.shard_map(
        gathered if small else exchanged,
        mesh=mesh, in_specs=in_specs, out_specs=out_specs, check_vma=False,
    )
```
